32 devices in a mesh: dev: 32 (over z, y, x, core).
Axes of the slice: x: 2, y: 2, z: 4, core: 2. Of those that a mesh axis runs over, the one named last changes fastest.
Arguments:
- left_table: float32 [65536, 256], P('dev'), may hold values from -6 to 6
- left_state: float32 [65536], P('dev'), may hold values from 0.001 to 0.1
- right_table: float32 [65536, 256], P('dev'), may hold values from -6 to 6
- right_state: float32 [65536], P('dev'), may hold values from 0.001 to 0.1
- relations: float32 [4, 256, 256], replicated, may hold values from -0.375 to 0.375
- relation_state: float32 [4, 256], replicated, may hold values from 819 to 81920
- edge_weights: int32 [32, 4, 16, 128, 128], P('dev'), may hold values from 0 to 3
- tile_left: int32 [32, 4, 16], P('dev'), may hold values from 0 to 15
- tile_right: int32 [32, 4, 16], P('dev'), may hold values from 0 to 15
- tile_relation: int32 [32, 4, 16], P('dev'), may hold values from 0 to 3
- live_count: int32 [32, 4], P('dev'), may hold values from 2 to 16, as said below
Outputs:
- left_out: float32 [65536, 256], P('dev')
- left_state_out: float32 [65536], P('dev')
- right_out: float32 [65536, 256], P('dev')
- right_state_out: float32 [65536], P('dev')
- relations_out: float32 [4, 256, 256], replicated
- relation_state_out: float32 [4, 256], replicated
The draws below stay inside these ranges and needn't reach their ends.
Inputs may be any that keep to these rules, and one draw needn't show every extreme that they name: `live_count`: in round 0 some partition has exactly 16 live slots.
All inputs are finite; a program needn't handle non-finite values.
Results may differ from the reference program's by a relative error of at most 0.0003.
Values sent between devices are 32-bit elements; how exact they have to be, the bound alone decides.
No kernel may reach another device: no remote copies, remote signals or barrier semaphores. Data moves between devices by JAX's collectives and lax.ppermute only.
A program may use at most 128 MiB of HBM per device.

```python
import math
import jax
import jax.numpy as jnp
from jax import lax

D = 256
RELS = 4
TILE = 128
ROWS = 2048
ROUNDS = 4
ACTIVE = 16
PARTITIONS = 32
TILES = 16
TABLE_ROWS = 65536


def draw_live_count(key, part):
    key_first, key_second, key_mark = jax.random.split(jax.random.fold_in(key, 17), 3)
    first = jax.random.randint(key_first, (PARTITIONS, ROUNDS), 0, ACTIVE)
    second = jax.random.randint(key_second, (PARTITIONS, ROUNDS), 0, ACTIVE)
    counted = 2 + (first * second + ACTIVE // 2) // ACTIVE
    counted = jnp.minimum(counted, ACTIVE)
    marked = jax.random.randint(key_mark, (), 0, PARTITIONS)
    spot = (jnp.arange(PARTITIONS)[:, None] == marked) & (jnp.arange(ROUNDS)[None, :] == 0)
    return jnp.where(spot, ACTIVE, counted).astype(jnp.int32)


def set_ends(drawn, stream_key, least, high):
    longest = drawn.shape.index(max(drawn.shape))
    spots = []
    for shift in (0, 1):
        where = [jax.random.randint(jax.random.fold_in(stream_key, axis), (), 0, length) for axis, length in enumerate(drawn.shape)]
        where[longest] = (where[longest] + shift) % drawn.shape[longest]
        spots.append(tuple(where))
    return drawn.at[spots[0]].set(least).at[spots[1]].set(high)


def block_scale(key, dims, shards, least, top_value):
    def one(dim, shards_of):
        draws = jax.random.uniform(jax.random.fold_in(jax.random.fold_in(key, 6), dim), (shards_of,), jnp.float32, least / len(shards), top_value / len(shards))
        return jnp.repeat(jnp.exp(draws), dims[dim] // shards_of).reshape((-1,) + (1,) * (len(dims) - dim - 1))

    level = one(*shards[0])
    for cut in shards[1:]:
        level = level * one(*cut)
    return level


def normal_values(stream_key, shape, width, reach, cuts=(), kind=jnp.bfloat16):
    values = jax.random.normal(stream_key, shape, jnp.float32) * width
    if len(cuts) > 0:
        values = block_scale(stream_key, shape, cuts, -0.22, 0.18) * values
    return jnp.clip(values, min=-reach, max=reach).astype(kind)


def setup_inputs(seed: int = 0) -> dict:
    splits = jax.random.split(jax.random.key(seed), 12)
    left_table = normal_values(splits[0], (TABLE_ROWS, D), 1.0, 6.0, ((0, 32),), jnp.float32)
    left_state = jnp.clip(jnp.exp(math.log(0.1) - 4.6051702 * jax.random.uniform(splits[1], (TABLE_ROWS,), jnp.float32) ** block_scale(splits[1], (TABLE_ROWS,), ((0, 32),), -0.2, 0.2)), 0.001, 0.1)
    right_table = normal_values(splits[2], (TABLE_ROWS, D), 1.0, 6.0, ((0, 32),), jnp.float32)
    right_state = jnp.clip(jnp.exp(math.log(0.1) - 4.6051702 * jax.random.uniform(splits[3], (TABLE_ROWS,), jnp.float32) ** block_scale(splits[3], (TABLE_ROWS,), ((0, 32),), -0.2, 0.2)), 0.001, 0.1)
    relations = normal_values(splits[4], (RELS, D, D), D ** -0.5, 0.375, (), jnp.float32)
    relation_state = jnp.clip(jnp.exp(jax.random.uniform(splits[5], (RELS, D), jnp.float32, math.log(819.0), math.log(81920.0))), 819.0, 81920.0)
    edge_weights = set_ends(jax.random.randint(splits[6], (PARTITIONS, ROUNDS, ACTIVE, TILE, TILE), 0, 4), jax.random.fold_in(splits[6], 1), 0, 3).astype(jnp.int32)
    tile_left = set_ends(jax.random.randint(splits[7], (PARTITIONS, ROUNDS, ACTIVE), 0, TILES), jax.random.fold_in(splits[7], 1), 0, TILES - 1).astype(jnp.int32)
    tile_right = set_ends(jax.random.randint(splits[8], (PARTITIONS, ROUNDS, ACTIVE), 0, TILES), jax.random.fold_in(splits[8], 1), 0, TILES - 1).astype(jnp.int32)
    tile_relation = set_ends(jax.random.randint(splits[9], (PARTITIONS, ROUNDS, ACTIVE), 0, RELS), jax.random.fold_in(splits[9], 1), 0, RELS - 1).astype(jnp.int32)
    live_count = draw_live_count(jax.random.fold_in(splits[11], 71), 0)
    return dict(left_table=left_table, left_state=left_state, right_table=right_table, right_state=right_state, relations=relations, relation_state=relation_state, edge_weights=edge_weights, tile_left=tile_left, tile_right=tile_right, tile_relation=tile_relation, live_count=live_count)


HIGHEST = lax.Precision.HIGHEST
learn_rate = 0.1
epsilon = 1e-06
weight_scale = 3.0

def slot_terms(rows_a, rows_b, relation_map, weights):
    scale = D ** (-0.5)
    projected = jnp.dot(rows_a, relation_map, precision=HIGHEST)
    scores = jnp.dot(projected, rows_b.T, precision=HIGHEST) * scale
    positive = weights.astype(scores.dtype) / weight_scale
    negative = (weights == 0).astype(scores.dtype)
    dscore = (negative * jax.nn.sigmoid(scores) - positive * jax.nn.sigmoid(-scores)) * scale
    term_b = jnp.dot(dscore.T, projected, precision=HIGHEST)
    backed = jnp.dot(dscore, rows_b, precision=HIGHEST)
    term_a = jnp.dot(backed, relation_map.T, precision=HIGHEST)
    term_rel = jnp.dot(rows_a.T, backed, precision=HIGHEST)
    return (term_a, term_b, term_rel)

def bucket_grads(table_a, table_b, relations, edges, lefts, rights, kinds, count):

    def add_slot(index, grads):
        grad_a, grad_b, grad_rel = grads
        start_a = (lefts[index] * TILE).astype(jnp.int32)
        start_b = (rights[index] * TILE).astype(jnp.int32)
        rows_a = lax.dynamic_slice_in_dim(table_a, start_a, TILE, 0)
        rows_b = lax.dynamic_slice_in_dim(table_b, start_b, TILE, 0)
        relation_map = lax.dynamic_index_in_dim(relations, kinds[index], 0, keepdims=False)
        term_a, term_b, term_rel = slot_terms(rows_a, rows_b, relation_map, edges[index])
        grad_a = lax.dynamic_update_slice_in_dim(grad_a, lax.dynamic_slice_in_dim(grad_a, start_a, TILE, 0) + term_a, start_a, 0)
        grad_b = lax.dynamic_update_slice_in_dim(grad_b, lax.dynamic_slice_in_dim(grad_b, start_b, TILE, 0) + term_b, start_b, 0)
        grad_rel = grad_rel.at[kinds[index]].add(term_rel)
        return (grad_a, grad_b, grad_rel)
    start = (jnp.zeros_like(table_a), jnp.zeros_like(table_b), jnp.zeros_like(relations))
    return lax.fori_loop(jnp.int32(0), count.astype(jnp.int32), add_slot, start)

def adagrad_rows(table, state, grad):
    state_new = state + lax.optimization_barrier(jnp.mean(grad * grad, axis=1))
    table_new = table - learn_rate * grad / (jnp.sqrt(state_new)[:, None] + epsilon)
    return (table_new, state_new)

def reference(left_table, left_state, right_table, right_state, relations, relation_state, edge_weights, tile_left, tile_right, tile_relation, live_count):
    lefts_all = left_table.reshape(PARTITIONS, ROWS, D)
    left_states = left_state.reshape(PARTITIONS, ROWS)
    rights_all = right_table.reshape(PARTITIONS, ROWS, D)
    right_states = right_state.reshape(PARTITIONS, ROWS)
    rel_grad = jnp.zeros_like(relations)
    for turn in range(ROUNDS):
        visiting = jnp.roll(rights_all, turn, axis=0)
        visiting_state = jnp.roll(right_states, turn, axis=0)

        def one_holder(total, items):
            table_a, state_a, table_b, state_b, edges, lefts, rights, kinds, count = items
            grad_a, grad_b, grad_rel = bucket_grads(table_a, table_b, relations, edges, lefts, rights, kinds, count)
            table_a, state_a = adagrad_rows(table_a, state_a, grad_a)
            table_b, state_b = adagrad_rows(table_b, state_b, grad_b)
            return (total + grad_rel, (table_a, state_a, table_b, state_b))
        items = (lefts_all, left_states, visiting, visiting_state, edge_weights[:, turn], tile_left[:, turn], tile_right[:, turn], tile_relation[:, turn], live_count[:, turn])
        rel_grad, results = lax.scan(one_holder, rel_grad, items)
        lefts_all, left_states, visiting, visiting_state = results
        rights_all = jnp.roll(visiting, -turn, axis=0)
        right_states = jnp.roll(visiting_state, -turn, axis=0)
    flat_rel, flat_state = adagrad_rows(relations.reshape(RELS * D, D), relation_state.reshape(RELS * D), rel_grad.reshape(RELS * D, D))
    return (lefts_all.reshape(TABLE_ROWS, D), left_states.reshape(TABLE_ROWS), rights_all.reshape(TABLE_ROWS, D), right_states.reshape(TABLE_ROWS), flat_rel.reshape(RELS, D, D), flat_state.reshape(RELS, D))
```

```python
import functools

import jax
import jax.numpy as jnp
from jax import lax
from jax.experimental import pallas as pl
from jax.experimental.pallas import tpu as pltpu
from jax.sharding import PartitionSpec as P

learn_rate = 0.1
epsilon = 1e-06
weight_scale = 3.0

F32 = jnp.float32
BF16 = jnp.bfloat16


def split(value):
    high = value.astype(BF16)
    return high, (value - high.astype(F32)).astype(BF16)


def dot3(a, b, dims):
    (ah, al), (bh, bl) = a, b
    d = functools.partial(lax.dot_general, dimension_numbers=(dims, ((), ())), preferred_element_type=F32)
    return d(ah, bh) + (d(ah, bl) + d(al, bh))


NN = ((1,), (0,))
NT = ((1,), (1,))
TN = ((0,), (0,))


def adagrad_tile(table, state_row, grad):
    tile = grad.shape[0]
    eye = lax.broadcasted_iota(jnp.int32, (tile, tile), 0) == lax.broadcasted_iota(jnp.int32, (tile, tile), 1)
    mean = jnp.sum(grad * grad, axis=1, keepdims=True) / grad.shape[1]
    mean_row = jnp.sum(jnp.where(eye, mean, 0.0), axis=0, keepdims=True)
    state_new = state_row + mean_row
    state_col = jnp.sum(jnp.where(eye, state_new, 0.0), axis=1, keepdims=True)
    return table - learn_rate * grad / (jnp.sqrt(state_col) + epsilon), state_new


def bucket_kernel(
    lefts, rights, kinds, count, edges, left, left_state, right, right_state, rel_high, rel_low, rel_in,
    left_out, left_state_out, right_out, right_state_out, rel_out, grad_a, grad_b, used,
):
    tiles, tile = left_state.shape
    width = left.shape[1]
    scale = width ** (-0.5)
    live = count[0]
    rel_out[...] = rel_in[...]
    for t in range(2 * tiles):
        used[t] = 0

    def slot(i, carry):
        ta, tb, kind = lefts[i], rights[i], kinds[i]
        ra = pl.ds(pl.multiple_of(ta * tile, tile), tile)
        rb = pl.ds(pl.multiple_of(tb * tile, tile), tile)

        @pl.when(used[ta] == 0)
        def _():
            grad_a[ra, :] = jnp.zeros((tile, width), F32)

        @pl.when(used[tiles + tb] == 0)
        def _():
            grad_b[rb, :] = jnp.zeros((tile, width), F32)

        used[ta] = 1
        used[tiles + tb] = 1
        a = split(left[ra, :])
        b = split(right[rb, :])
        m = (rel_high[kind], rel_low[kind])
        p = split(dot3(a, m, NN))
        s = dot3(p, b, NT) * scale
        w = edges[i]
        sig = jax.nn.sigmoid(s)
        pos = w.astype(F32) / weight_scale
        g = split((jnp.where(w == 0, sig, 0.0) - pos * jax.nn.sigmoid(-s)) * scale)
        back = split(dot3(g, b, NN))
        grad_b[rb, :] += dot3(g, p, TN)
        grad_a[ra, :] += dot3(back, m, NT)
        rel_out[kind] += dot3(a, back, TN)
        return carry

    lax.fori_loop(0, live, slot, 0)
    left_state_out[...] = left_state[...]
    right_state_out[...] = right_state[...]

    def update(t, carry):
        rows = pl.ds(pl.multiple_of(t * tile, tile), tile)
        for at, table, state, table_out, state_out, grad in (
            (0, left, left_state, left_out, left_state_out, grad_a),
            (tiles, right, right_state, right_out, right_state_out, grad_b),
        ):
            @pl.when(used[at + t] == 0)
            def _():
                table_out[rows, :] = table[rows, :]

            @pl.when(used[at + t] != 0)
            def _():
                new, state_new = adagrad_tile(table[rows, :], state[pl.ds(t, 1), :], grad[rows, :])
                table_out[rows, :] = new
                state_out[pl.ds(t, 1), :] = state_new

        return carry

    lax.fori_loop(0, tiles, update, 0)


def run_bucket(edges, lefts, rights, kinds, count, left, left_state, right, right_state, rel_high, rel_low, rel):
    vmem = pl.BlockSpec(memory_space=pltpu.VMEM)
    smem = pl.BlockSpec(memory_space=pltpu.SMEM)
    like = lambda x: jax.ShapeDtypeStruct(x.shape, x.dtype)
    slots, tile = edges.shape[0], edges.shape[1]
    width = left.shape[1]
    flops = 6 * slots * tile * width * (3 * width + 3 * tile)
    return pl.pallas_call(
        bucket_kernel,
        in_specs=[smem] * 4 + [vmem] * 8,
        out_specs=[vmem] * 5,
        out_shape=[like(left), like(left_state), like(right), like(right_state), like(rel)],
        scratch_shapes=[
            pltpu.VMEM(left.shape, F32),
            pltpu.VMEM(right.shape, F32),
            pltpu.SMEM((2 * left_state.shape[0],), jnp.int32),
        ],
        compiler_params=pltpu.CompilerParams(vmem_limit_bytes=48 * 1024 * 1024),
        cost_estimate=pl.CostEstimate(flops=flops, bytes_accessed=12 * left.size, transcendentals=0),
    )(lefts, rights, kinds, count, edges, left, left_state, right, right_state, rel_high, rel_low, rel)


def shifted(block, axis, distance):
    n = lax.axis_size(axis)
    return lax.ppermute(block, axis, [((i - distance) % n, i) for i in range(n)])


def sum_over(block, axis):
    n = lax.axis_size(axis)
    me = lax.axis_index(axis)
    bits = n.bit_length() - 1
    if n != 1 << bits or block.shape[0] % n:
        return lax.psum(block, axis)
    for b in range(bits):
        mine = ((me >> b) & 1) == 1
        half = block.shape[0] // 2
        low, high = block[:half], block[half:]
        got = lax.ppermute(jnp.where(mine, low, high), axis, [(i, i ^ (1 << b)) for i in range(n)])
        block = jnp.where(mine, high, low) + got
    for b in reversed(range(bits)):
        mine = ((me >> b) & 1) == 1
        got = lax.ppermute(block, axis, [(i, i ^ (1 << b)) for i in range(n)])
        block = jnp.concatenate([jnp.where(mine, got, block), jnp.where(mine, block, got)])
    return block


def adagrad_rows(table, state, grad):
    state_new = state + jnp.mean(grad * grad, axis=1)
    return table - learn_rate * grad / (jnp.sqrt(state_new)[:, None] + epsilon), state_new


def per_device(
    left_table, left_state, right_table, right_state, relations, relation_state,
    edge_weights, tile_left, tile_right, tile_relation, live_count,
):
    edges, lefts, rights, kinds, counts = (
        edge_weights[0], tile_left[0], tile_right[0], tile_relation[0], live_count[0],
    )
    rounds, tile = edges.shape[0], edges.shape[-1]
    rounded = lax.reduce_precision(relations, 8, 7)
    rel_high, rel_low = rounded.astype(BF16), (relations - rounded).astype(BF16)
    rel = jnp.zeros_like(relations)
    left, right = left_table, right_table
    state_l, state_r = left_state.reshape(-1, tile), right_state.reshape(-1, tile)
    for turn in range(rounds):
        left, state_l, right, state_r, rel = run_bucket(
            edges[turn], lefts[turn], rights[turn], kinds[turn], counts[turn : turn + 1],
            left, state_l, right, state_r, rel_high, rel_low, rel,
        )
        if turn + 1 < rounds:
            right, state_r = shifted((right, state_r), "dev", 1)
    right, state_r = shifted((right, state_r), "dev", -(rounds - 1))
    width = relations.shape[-1]
    total = sum_over(rel.reshape(-1, width), "dev")
    new_rel, new_state = adagrad_rows(relations.reshape(-1, width), relation_state.reshape(-1), total)
    return (
        left, state_l.reshape(left_state.shape), right, state_r.reshape(right_state.shape),
        new_rel.reshape(relations.shape), new_state.reshape(relation_state.shape),
    )


def solution(mesh):
    placed = (
        P("dev", None), P("dev"), P("dev", None), P("dev"), P(), P(),
        P("dev", None, None, None, None), P("dev", None, None), P("dev", None, None), P("dev", None, None),
        P("dev", None),
    )
    return jax.shard_map(
        per_device, mesh=mesh, in_specs=placed,
        out_specs=(P("dev", None), P("dev"), P("dev", None), P("dev"), P(), P()), check_vma=False,
    )
```

```python
import functools

import jax
import jax.numpy as jnp
from jax import lax
from jax.experimental import pallas as pl
from jax.experimental.pallas import tpu as pltpu
from jax.sharding import PartitionSpec as P

learn_rate = 0.1
epsilon = 1e-06
weight_scale = 3.0

F32 = jnp.float32
BF16 = jnp.bfloat16
PARTS = 2
TOGETHER = 2
UPDATES = 4

NN = ((1,), (0,))
NT = ((1,), (1,))
TN = ((0,), (0,))


def split(value):
    high = value.astype(BF16)
    return high, (value - high.astype(F32)).astype(BF16)


def dot3(a, b, dims):
    (ah, al), (bh, bl) = a, b
    ca, cb = dims[0][0], dims[1][0]
    return lax.dot_general(
        jnp.concatenate([ah, ah, al], axis=ca),
        jnp.concatenate([bh, bl, bh], axis=cb),
        (dims, ((), ())),
        preferred_element_type=F32,
    )


def dscore(s, w, scale):
    small = jnp.exp(-jnp.abs(s))
    large_part = 1.0 / (1.0 + small)
    small_part = small * large_part
    up = s >= 0
    sig = jnp.where(up, large_part, small_part)
    anti = jnp.where(up, small_part, large_part)
    return jnp.where(w == 0, sig, anti * (w.astype(F32) * (-1.0 / weight_scale))) * scale


def adagrad_tile(table, state_row, grad):
    tile, width = grad.shape
    eye = lax.broadcasted_iota(jnp.int32, (tile, tile), 0) == lax.broadcasted_iota(jnp.int32, (tile, tile), 1)
    mean = jnp.sum(grad * grad, axis=1, keepdims=True) / width
    state_new = state_row + jnp.sum(jnp.where(eye, mean, 0.0), axis=0, keepdims=True)
    rate_row = learn_rate / (jnp.sqrt(state_new) + epsilon)
    rate = jnp.sum(jnp.where(eye, rate_row, 0.0), axis=1, keepdims=True)
    return table - grad * rate, state_new


def bucket_kernel(turn, part, first, dims, lefts, rights, kinds, count, edges, *refs):
    tiles, per_part, tile, width, kinds_count = dims
    last = part == PARTS - 1
    refs = list(refs)
    left = refs.pop(0)
    state_l = refs.pop(0) if last else None
    right = refs.pop(0)
    state_r = refs.pop(0) if first else None
    operators = refs.pop(0)
    rel = None if first and part == 0 else refs.pop(0)
    handed = refs.pop(0) if last else None
    if last:
        left_out, state_l_out = refs.pop(0), refs.pop(0)
    right_out, rel_out = refs.pop(0), refs.pop(0)
    handed_out = None if last else refs.pop(0)
    (weights, held, grads, states, maps, highs, lows, grad_r, seen, order, todo, sem_w, sem_t, sem_g, sem_k, sem_s) = refs
    fill = first and last
    scale = width ** (-0.5)
    live = count[0, turn]
    spare = tiles + per_part
    kind_at = spare

    def rows(t):
        return pl.ds(pl.multiple_of(t * tile, tile), tile)

    def load_left(t):
        return pltpu.make_async_copy(left.at[rows(t)], held.at[rows(t)], sem_t.at[t])

    def store_left(t):
        return pltpu.make_async_copy(held.at[rows(t)], left_out.at[rows(t)], sem_t.at[t])

    def load_right(t):
        at = tiles + t
        source = right.at[rows(part * per_part + t)] if first else right.at[rows(t)]
        return pltpu.make_async_copy(source, held.at[rows(at)], sem_t.at[at])

    def store_right(t):
        at = tiles + t
        return pltpu.make_async_copy(held.at[rows(at)], right_out.at[rows(t)], sem_t.at[at])

    def take(t):
        return pltpu.make_async_copy(handed.at[rows(t)], grads.at[rows(t)], sem_g.at[t])

    def hand(t):
        return pltpu.make_async_copy(grads.at[rows(t)], handed_out.at[rows(t)], sem_g.at[t])

    def load_weights(i):
        return pltpu.make_async_copy(edges.at[0, turn, i], weights.at[i], sem_w.at[i])

    def load_kind(kind):
        copies = [pltpu.make_async_copy(operators.at[kind], maps.at[kind], sem_k.at[0, kind])]
        if rel is not None:
            copies.append(pltpu.make_async_copy(rel.at[kind], grad_r.at[kind], sem_k.at[1, kind]))
        return copies

    def store_kind(kind):
        return pltpu.make_async_copy(grad_r.at[kind], rel_out.at[kind], sem_k.at[1, kind])

    held_r = states.at[pl.ds(tiles, per_part)]
    packed = pl.ds(per_part * tile, per_part), pl.ds(0, tile)
    source = state_r.at[pl.ds(part * per_part, per_part)] if first else right.at[packed]
    load_states = [pltpu.make_async_copy(source, held_r, sem_s.at[0])]
    store_states = [pltpu.make_async_copy(held_r, right_out.at[packed], sem_s.at[0])]
    if last:
        held_l = states.at[pl.ds(0, tiles)]
        load_states.append(pltpu.make_async_copy(state_l, held_l, sem_s.at[1]))
        store_states.append(pltpu.make_async_copy(held_l, state_l_out, sem_s.at[1]))

    for t in range(spare + kinds_count):
        seen[t] = 0
    for t in range(spare + UPDATES):
        order[t] = spare
    used = jnp.int32(0)

    def mine(i):
        return rights[0, turn, i] // per_part == part

    def ask(i, carry):
        used, jobs = carry
        now = mine(i)
        a, b, kind = lefts[0, turn, i], rights[0, turn, i] - part * per_part, kinds[0, turn, i]
        new_a = now & (seen[a] == 0)
        new_b = now & (seen[jnp.where(now, tiles + b, 0)] == 0)

        @pl.when(now)
        def _():
            todo[jobs] = i
            load_weights(i).start()

            @pl.when(seen[kind_at + kind] == 0)
            def _():
                for copy in load_kind(kind):
                    copy.start()
                seen[kind_at + kind] = 1

        @pl.when(new_a)
        def _():
            load_left(a).start()
            seen[a] = 1
            grads[rows(a), :] = jnp.zeros((tile, width), F32)
            if last:
                order[used] = a

        if last:
            used = used + new_a.astype(jnp.int32)

        @pl.when(new_b)
        def _():
            load_right(b).start()
            seen[tiles + b] = 1
            grads[rows(tiles + b), :] = jnp.zeros((tile, width), F32)
            order[used] = tiles + b

        return used + new_b.astype(jnp.int32), jobs + now.astype(jnp.int32)

    if last:
        def ask_handed(i, used):
            a = lefts[0, turn, i]
            new = jnp.logical_not(mine(i)) & (seen[a] == 0)

            @pl.when(new)
            def _():
                load_left(a).start()
                take(a).start()
                seen[a] = 4
                order[used] = a

            return used + new.astype(jnp.int32)

        used = lax.fori_loop(0, live, ask_handed, used)
    used, jobs = lax.fori_loop(0, live, ask, (used, jnp.int32(0)))
    states[pl.ds(spare, 8), :] = jnp.ones((8, tile), F32)
    for copy in load_states:
        copy.start()
    if rel is None:
        grad_r[...] = jnp.zeros_like(grad_r)

    def each_unseen(side_count, base, act):
        def body(t, carry):
            pl.when(seen[base + t] == 0)(lambda: act(t))
            return carry

        lax.fori_loop(0, side_count, body, 0)

    if fill:
        each_unseen(tiles, 0, lambda t: load_left(t).start())
    if first:
        each_unseen(per_part, tiles, lambda t: load_right(t).start())
    held[rows(spare), :] = jnp.zeros((tile, width), F32)
    grads[rows(spare), :] = jnp.zeros((tile, width), F32)

    def arrive_left(a):
        @pl.when(seen[a] == 1)
        def _():
            load_left(a).wait()
            seen[a] = 2

        if last:
            @pl.when(seen[a] == 4)
            def _():
                load_left(a).wait()
                take(a).wait()
                seen[a] = 2

    def arrive(i):
        arrive_left(lefts[0, turn, i])
        b, kind = rights[0, turn, i] - part * per_part, kinds[0, turn, i]

        @pl.when(seen[tiles + b] == 1)
        def _():
            load_right(b).wait()
            seen[tiles + b] = 2

        @pl.when(seen[kind_at + kind] == 1)
        def _():
            for copy in load_kind(kind):
                copy.wait()
            highs[kind], lows[kind] = split(maps[kind])
            seen[kind_at + kind] = 2

        load_weights(i).wait()

    def group(j, carry):
        places = [j * TOGETHER + n for n in range(TOGETHER)]
        slots = [todo[jnp.minimum(place, jobs - 1)] for place in places]
        arrive(slots[0])
        for i, place in zip(slots[1:], places[1:]):
            pl.when(place < jobs)(functools.partial(arrive, i))
        work = [
            (
                jnp.where(place < jobs, lefts[0, turn, i], spare),
                jnp.where(place < jobs, tiles + rights[0, turn, i] - part * per_part, spare),
                kinds[0, turn, i],
            )
            for i, place in zip(slots, places)
        ]
        a = [split(held[rows(ta), :]) for ta, _, _ in work]
        b = [split(held[rows(tb), :]) for _, tb, _ in work]
        m = [(highs[kind], lows[kind]) for _, _, kind in work]
        p = [split(dot3(x, y, NN)) for x, y in zip(a, m)]
        s = [dot3(x, y, NT) * scale for x, y in zip(p, b)]
        g = [split(dscore(x, weights[i], scale)) for x, i in zip(s, slots)]
        back = [split(dot3(x, y, NN)) for x, y in zip(g, b)]
        term_b = [dot3(x, y, TN) for x, y in zip(g, p)]
        term_a = [dot3(x, y, NT) for x, y in zip(back, m)]
        term_r = [dot3(x, y, TN) for x, y in zip(a, back)]
        for (ta, tb, kind), x, y, z in zip(work, term_a, term_b, term_r):
            grads[rows(ta), :] += x
            grads[rows(tb), :] += y
            grad_r[kind] += z
        return carry

    lax.fori_loop(0, (jobs + TOGETHER - 1) // TOGETHER, group, 0)

    def each_kind(act):
        for kind in range(kinds_count):
            if rel is None:
                act(store_kind(kind))
            else:
                pl.when(seen[kind_at + kind] == 2)(functools.partial(act, store_kind(kind)))

    each_kind(lambda copy: copy.start())
    if first:
        each_unseen(per_part, tiles, lambda t: (load_right(t).wait(), store_right(t).start()) and None)
    if last:
        def settle_handed(t, carry):
            arrive_left(t)
            return carry

        lax.fori_loop(0, tiles, settle_handed, 0)
        if fill:
            each_unseen(tiles, 0, lambda t: (load_left(t).wait(), store_left(t).start()) and None)

    for copy in load_states:
        copy.wait()

    def update(j, carry):
        places = [order[j * UPDATES + n] for n in range(UPDATES)]
        done = [adagrad_tile(held[rows(at), :], states[pl.ds(at, 1), :], grads[rows(at), :]) for at in places]
        for at, (new, state_new) in zip(places, done):
            held[rows(at), :] = new
            states[pl.ds(at, 1), :] = state_new
            if last:
                pl.when(at < tiles)(lambda: store_left(at).start())
            pl.when((at >= tiles) & (at < spare))(lambda: store_right(at - tiles).start())
        return carry

    def each_touched(side_count, base, act):
        def body(t, carry):
            pl.when(seen[base + t] == 2)(lambda: act(t))
            return carry

        lax.fori_loop(0, side_count, body, 0)

    if not last:
        each_touched(tiles, 0, lambda t: hand(t).start())
    lax.fori_loop(0, (used + UPDATES - 1) // UPDATES, update, 0)
    for copy in store_states:
        copy.start()
    if not last:
        each_touched(tiles, 0, lambda t: hand(t).wait())
    else:
        each_touched(tiles, 0, lambda t: store_left(t).wait())
    each_touched(per_part, tiles, lambda t: store_right(t).wait())
    if fill:
        each_unseen(tiles, 0, lambda t: store_left(t).wait())
    if first:
        each_unseen(per_part, tiles, lambda t: store_right(t).wait())
    for copy in store_states:
        copy.wait()
    each_kind(lambda copy: copy.wait())


def run_part(turn, part, edges, lefts, rights, kinds, count, left, state_l, right, state_r, operators, rel, handed):
    first, last = state_r is not None, part == PARTS - 1
    anywhere = pl.BlockSpec(memory_space=pl.ANY)
    smem = pl.BlockSpec(memory_space=pltpu.SMEM)
    slots, tile = edges.shape[2], edges.shape[3]
    tiles, width = state_l.shape[0], left.shape[1]
    per_part = tiles // PARTS
    kinds_count = operators.shape[0]
    rows = (tiles + per_part + 1) * tile
    dma = pltpu.SemaphoreType.DMA
    shape = lambda *dims: jax.ShapeDtypeStruct(dims, F32)
    names = [("lefts", lefts), ("rights", rights), ("kinds", kinds), ("count", count), ("edges", edges), ("left", left)]
    names += [("state_l", state_l)] if last else []
    names += [("right", right)]
    names += [("state_r", state_r)] if first else []
    names += [("operators", operators)]
    names += [("rel", rel)] if rel is not None else []
    names += [("handed", handed)] if last else []
    outs = [("left", shape(*left.shape)), ("state_l", shape(*state_l.shape))] if last else []
    outs += [("right", shape(per_part * (tile + 1), width)), ("rel", shape(*operators.shape))]
    outs += [] if last else [("handed", shape(*left.shape))]
    place = {name: i for i, (name, _) in enumerate(names)}
    shared = {
        place[name]: i for i, (name, _) in enumerate(outs)
        if name in place and (name == "rel" or not first)
    }
    new = pl.pallas_call(
        functools.partial(bucket_kernel, turn, part, first, (tiles, per_part, tile, width, kinds_count)),
        in_specs=[smem] * 4 + [anywhere] * (len(names) - 4),
        out_specs=[anywhere] * len(outs),
        out_shape=[out for _, out in outs],
        input_output_aliases=shared,
        scratch_shapes=[
            pltpu.VMEM((slots, tile, tile), jnp.int32),
            pltpu.VMEM((rows, width), F32),
            pltpu.VMEM((rows, width), F32),
            pltpu.VMEM((tiles + per_part + 8, tile), F32),
            pltpu.VMEM(operators.shape, F32),
            pltpu.VMEM(operators.shape, BF16),
            pltpu.VMEM(operators.shape, BF16),
            pltpu.VMEM(operators.shape, F32),
            pltpu.SMEM((tiles + per_part + kinds_count,), jnp.int32),
            pltpu.SMEM((tiles + per_part + UPDATES,), jnp.int32),
            pltpu.SMEM((slots,), jnp.int32),
            dma((slots,)),
            dma((tiles + per_part,)),
            dma((tiles,)),
            dma((2, kinds_count)),
            dma((2,)),
        ],
        compiler_params=pltpu.CompilerParams(vmem_limit_bytes=60 * 1024 * 1024),
        cost_estimate=pl.CostEstimate(flops=4 * 10**9, bytes_accessed=4 * left.size, transcendentals=0),
    )(*[value for _, value in names])
    return dict(zip([name for name, _ in outs], new))


def unpack_kernel(*refs):
    parts, (table, state), (sems,) = refs[:PARTS], refs[PARTS : PARTS + 2], refs[PARTS + 2 :]
    body = table.shape[0] // PARTS
    per_part, tile = state.shape[0] // PARTS, state.shape[1]
    copies = []
    for n, part in enumerate(parts):
        copies.append(
            pltpu.make_async_copy(part.at[pl.ds(0, body)], table.at[pl.ds(n * body, body)], sems.at[2 * n])
        )
        copies.append(
            pltpu.make_async_copy(
                part.at[pl.ds(body, per_part), pl.ds(0, tile)], state.at[pl.ds(n * per_part, per_part)],
                sems.at[2 * n + 1],
            )
        )
    for copy in copies:
        copy.start()
    for copy in copies:
        copy.wait()


def unpack(parts, table, state):
    return pl.pallas_call(
        unpack_kernel,
        in_specs=[pl.BlockSpec(memory_space=pltpu.VMEM)] * PARTS,
        out_specs=[pl.BlockSpec(memory_space=pl.ANY)] * 2,
        out_shape=[jax.ShapeDtypeStruct(table, F32), jax.ShapeDtypeStruct(state, F32)],
        scratch_shapes=[pltpu.SemaphoreType.DMA((2 * PARTS,))],
        compiler_params=pltpu.CompilerParams(vmem_limit_bytes=16 * 1024 * 1024),
    )(*parts)


def shifted(block, axis, distance):
    n = lax.axis_size(axis)
    return lax.ppermute(block, axis, [(i, (i + distance) % n) for i in range(n)])


def sum_over(block, axis, sends, distance):
    n = lax.axis_size(axis)
    bits = n.bit_length() - 1
    if n != 1 << bits or block.shape[0] % n:
        return lax.psum(block, axis), [shifted(x, axis, distance) for x in sends]
    me = lax.axis_index(axis)
    digits, at = [], 0
    while at < bits:
        wide = 1 if at == 0 else min(2, bits - at)
        digits.append((at, 1 << wide))
        at += wide
    sends, arrived = list(sends), {0: shifted(sends[0], axis, distance)}
    plan = iter([((), ()), ((), (0,)), ((1,), ()), ((), ()), ((), (1,))])

    def tie(block):
        send, want = next(plan, ((), ()))
        for which in send:
            block, sends[which] = lax.optimization_barrier((block, sends[which]))
            arrived[which] = shifted(sends[which], axis, distance)
        for which in want:
            block, arrived[which] = lax.optimization_barrier((block, arrived[which]))
        return block

    for at, size in digits:
        block = tie(block)
        mine = (me >> at) & (size - 1)
        parts = block.reshape(size, -1, block.shape[1])
        got = [
            lax.ppermute(
                lax.dynamic_index_in_dim(parts, mine ^ j, keepdims=False), axis,
                [(i, i ^ (j << at)) for i in range(n)],
            )
            for j in range(1, size)
        ]
        block = lax.dynamic_index_in_dim(parts, mine, keepdims=False)
        for other in got:
            block = block + other
    for at, size in reversed(digits):
        block = tie(block)
        mine = (me >> at) & (size - 1)
        got = [block] + [lax.ppermute(block, axis, [(i, i ^ (j << at)) for i in range(n)]) for j in range(1, size)]
        whole = jnp.zeros((size,) + block.shape, block.dtype)
        for j, other in enumerate(got):
            whole = lax.dynamic_update_index_in_dim(whole, other, mine ^ j, 0)
        block = whole.reshape(-1, block.shape[1])
    tie(block)
    return block, [arrived.get(i) if i in arrived else shifted(x, axis, distance) for i, x in enumerate(sends)]


def adagrad_rows(table, state, grad):
    state_new = state + jnp.mean(grad * grad, axis=1)
    return table - learn_rate * grad / (jnp.sqrt(state_new)[:, None] + epsilon), state_new


def per_device(
    left_table, left_state, right_table, right_state, relations, relation_state,
    edge_weights, tile_left, tile_right, tile_relation, live_count,
):
    rounds, tile = edge_weights.shape[1], edge_weights.shape[-1]
    left, state_l = left_table, left_state.reshape(-1, tile)
    rights_now = [right_table] * PARTS
    state_r = right_state.reshape(-1, tile)
    rel = None
    for turn in range(rounds):
        handed = None
        for part in range(PARTS):
            new = run_part(
                turn, part, edge_weights, tile_left, tile_right, tile_relation, live_count,
                left, state_l, rights_now[part], state_r if turn == 0 else None, relations, rel, handed,
            )
            rel, handed = new["rel"], new.get("handed")
            rights_now[part] = shifted(new["right"], "dev", 1) if turn + 1 < rounds else new["right"]
        left, state_l = new["left"], new["state_l"]
    width = relations.shape[-1]
    total, rights_now = sum_over(rel.reshape(-1, width), "dev", rights_now, 1 - rounds)
    right, state_r = unpack(rights_now, right_table.shape, (right_state.shape[0] // tile, tile))
    new_rel, new_state = adagrad_rows(relations.reshape(-1, width), relation_state.reshape(-1), total)
    return (
        left, state_l.reshape(left_state.shape), right, state_r.reshape(right_state.shape),
        new_rel.reshape(relations.shape), new_state.reshape(relation_state.shape),
    )


def solution(mesh):
    placed = (
        P("dev", None), P("dev"), P("dev", None), P("dev"), P(), P(),
        P("dev", None, None, None, None), P("dev", None, None), P("dev", None, None), P("dev", None, None),
        P("dev", None),
    )
    return jax.shard_map(
        per_device, mesh=mesh, in_specs=placed,
        out_specs=(P("dev", None), P("dev"), P("dev", None), P("dev"), P(), P()), check_vma=False,
    )
```

```python
import functools

import jax
import jax.numpy as jnp
from jax import lax
from jax.experimental import pallas as pl
from jax.experimental.pallas import tpu as pltpu
from jax.sharding import PartitionSpec as P

learn_rate = 0.1
epsilon = 1e-06
weight_scale = 3.0

F32 = jnp.float32
BF16 = jnp.bfloat16
PARTS = 2
TOGETHER = 4
UPDATES = 8

NN = ((1,), (0,))
NT = ((1,), (1,))
TN = ((0,), (0,))


def split(value):
    high = value.astype(BF16)
    return high, (value - high.astype(F32)).astype(BF16)


def dot3(a, b, dims):
    (ah, al), (bh, bl) = a, b
    ca, cb = dims[0][0], dims[1][0]
    return lax.dot_general(
        jnp.concatenate([ah, ah, al], axis=ca),
        jnp.concatenate([bh, bl, bh], axis=cb),
        (dims, ((), ())),
        preferred_element_type=F32,
    )


def dscore(s, w, scale):
    small = jnp.exp(-jnp.abs(s))
    large_part = 1.0 / (1.0 + small)
    small_part = small * large_part
    up = s >= 0
    sig = jnp.where(up, large_part, small_part)
    anti = jnp.where(up, small_part, large_part)
    return jnp.where(w == 0, sig, anti * (w.astype(F32) * (-1.0 / weight_scale))) * scale


def adagrad_tile(table, state_row, grad):
    tile, width = grad.shape
    eye = lax.broadcasted_iota(jnp.int32, (tile, tile), 0) == lax.broadcasted_iota(jnp.int32, (tile, tile), 1)
    mean = jnp.sum(grad * grad, axis=1, keepdims=True) / width
    state_new = state_row + jnp.sum(jnp.where(eye, mean, 0.0), axis=0, keepdims=True)
    rate_row = learn_rate / (jnp.sqrt(state_new) + epsilon)
    rate = jnp.sum(jnp.where(eye, rate_row, 0.0), axis=1, keepdims=True)
    return table - grad * rate, state_new


def bucket_kernel(turn, part, first, dims, lefts, rights, kinds, count, edges, *refs):
    tiles, per_part, tile, width, kinds_count = dims
    last = part == PARTS - 1
    refs = list(refs)
    left = refs.pop(0)
    state_l = refs.pop(0) if last else None
    right = refs.pop(0)
    state_r = refs.pop(0) if first else None
    operators = refs.pop(0)
    rel = None if first and part == 0 else refs.pop(0)
    handed = refs.pop(0) if last else None
    if last:
        left_out, state_l_out = refs.pop(0), refs.pop(0)
    right_out, rel_out = refs.pop(0), refs.pop(0)
    handed_out = None if last else refs.pop(0)
    (weights, held, grads, states, maps, highs, lows, grad_r, seen, order, todo, sem_w, sem_t, sem_g, sem_k, sem_s) = refs
    fill = first and last
    scale = width ** (-0.5)
    live = count[0, turn]
    spare = tiles + per_part
    kind_at = spare

    def rows(t):
        return pl.ds(pl.multiple_of(t * tile, tile), tile)

    def load_left(t):
        return pltpu.make_async_copy(left.at[rows(t)], held.at[rows(t)], sem_t.at[t])

    def store_left(t):
        return pltpu.make_async_copy(held.at[rows(t)], left_out.at[rows(t)], sem_t.at[t])

    def load_right(t):
        at = tiles + t
        source = right.at[rows(part * per_part + t)] if first else right.at[rows(t)]
        return pltpu.make_async_copy(source, held.at[rows(at)], sem_t.at[at])

    def store_right(t):
        at = tiles + t
        return pltpu.make_async_copy(held.at[rows(at)], right_out.at[rows(t)], sem_t.at[at])

    def take(t):
        return pltpu.make_async_copy(handed.at[rows(t)], grads.at[rows(t)], sem_g.at[t])

    def hand(t):
        return pltpu.make_async_copy(grads.at[rows(t)], handed_out.at[rows(t)], sem_g.at[t])

    def load_weights(i):
        return pltpu.make_async_copy(edges.at[0, turn, i], weights.at[i], sem_w.at[i])

    def load_kind(kind):
        copies = [pltpu.make_async_copy(operators.at[kind], maps.at[kind], sem_k.at[0, kind])]
        if rel is not None:
            copies.append(pltpu.make_async_copy(rel.at[kind], grad_r.at[kind], sem_k.at[1, kind]))
        return copies

    def store_kind(kind):
        return pltpu.make_async_copy(grad_r.at[kind], rel_out.at[kind], sem_k.at[1, kind])

    held_r = states.at[pl.ds(tiles, per_part)]
    packed = pl.ds(per_part * tile, per_part), pl.ds(0, tile)
    source = state_r.at[pl.ds(part * per_part, per_part)] if first else right.at[packed]
    load_states = [pltpu.make_async_copy(source, held_r, sem_s.at[0])]
    store_states = [pltpu.make_async_copy(held_r, right_out.at[packed], sem_s.at[0])]
    if last:
        held_l = states.at[pl.ds(0, tiles)]
        load_states.append(pltpu.make_async_copy(state_l, held_l, sem_s.at[1]))
        store_states.append(pltpu.make_async_copy(held_l, state_l_out, sem_s.at[1]))

    for t in range(spare + kinds_count):
        seen[t] = 0
    for t in range(spare + UPDATES):
        order[t] = spare
    used = jnp.int32(0)

    def mine(i):
        return rights[0, turn, i] // per_part == part

    def ask(i, carry):
        used, jobs = carry
        now = mine(i)
        a, b, kind = lefts[0, turn, i], rights[0, turn, i] - part * per_part, kinds[0, turn, i]
        new_a = now & (seen[a] == 0)
        new_b = now & (seen[jnp.where(now, tiles + b, 0)] == 0)

        @pl.when(now)
        def _():
            todo[jobs] = i
            load_weights(i).start()

            @pl.when(seen[kind_at + kind] == 0)
            def _():
                for copy in load_kind(kind):
                    copy.start()
                seen[kind_at + kind] = 1

        @pl.when(new_a)
        def _():
            load_left(a).start()
            seen[a] = 1
            grads[rows(a), :] = jnp.zeros((tile, width), F32)
            if last:
                order[used] = a

        if last:
            used = used + new_a.astype(jnp.int32)

        @pl.when(new_b)
        def _():
            load_right(b).start()
            seen[tiles + b] = 1
            grads[rows(tiles + b), :] = jnp.zeros((tile, width), F32)
            order[used] = tiles + b

        return used + new_b.astype(jnp.int32), jobs + now.astype(jnp.int32)

    if last:
        def ask_handed(i, used):
            a = lefts[0, turn, i]
            new = jnp.logical_not(mine(i)) & (seen[a] == 0)

            @pl.when(new)
            def _():
                load_left(a).start()
                take(a).start()
                seen[a] = 4
                order[used] = a

            return used + new.astype(jnp.int32)

        used = lax.fori_loop(0, live, ask_handed, used)
    used, jobs = lax.fori_loop(0, live, ask, (used, jnp.int32(0)))
    states[pl.ds(spare, 8), :] = jnp.ones((8, tile), F32)
    for copy in load_states:
        copy.start()
    if rel is None:
        grad_r[...] = jnp.zeros_like(grad_r)

    def each_unseen(side_count, base, act):
        def body(t, carry):
            pl.when(seen[base + t] == 0)(lambda: act(t))
            return carry

        lax.fori_loop(0, side_count, body, 0)

    if fill:
        each_unseen(tiles, 0, lambda t: load_left(t).start())
    if first:
        each_unseen(per_part, tiles, lambda t: load_right(t).start())
    held[rows(spare), :] = jnp.zeros((tile, width), F32)
    grads[rows(spare), :] = jnp.zeros((tile, width), F32)

    def arrive_left(a):
        @pl.when(seen[a] == 1)
        def _():
            load_left(a).wait()
            seen[a] = 2

        if last:
            @pl.when(seen[a] == 4)
            def _():
                load_left(a).wait()
                take(a).wait()
                seen[a] = 2

    def arrive(i):
        arrive_left(lefts[0, turn, i])
        b, kind = rights[0, turn, i] - part * per_part, kinds[0, turn, i]

        @pl.when(seen[tiles + b] == 1)
        def _():
            load_right(b).wait()
            seen[tiles + b] = 2

        @pl.when(seen[kind_at + kind] == 1)
        def _():
            for copy in load_kind(kind):
                copy.wait()
            highs[kind], lows[kind] = split(maps[kind])
            seen[kind_at + kind] = 2

        load_weights(i).wait()

    def group(j, carry):
        places = [j * TOGETHER + n for n in range(TOGETHER)]
        slots = [todo[jnp.minimum(place, jobs - 1)] for place in places]
        arrive(slots[0])
        for i, place in zip(slots[1:], places[1:]):
            pl.when(place < jobs)(functools.partial(arrive, i))
        work = [
            (
                jnp.where(place < jobs, lefts[0, turn, i], spare),
                jnp.where(place < jobs, tiles + rights[0, turn, i] - part * per_part, spare),
                kinds[0, turn, i],
            )
            for i, place in zip(slots, places)
        ]
        a = [split(held[rows(ta), :]) for ta, _, _ in work]
        b = [split(held[rows(tb), :]) for _, tb, _ in work]
        m = [(highs[kind], lows[kind]) for _, _, kind in work]
        p = [split(dot3(x, y, NN)) for x, y in zip(a, m)]
        s = [dot3(x, y, NT) * scale for x, y in zip(p, b)]
        g = [split(dscore(x, weights[i], scale)) for x, i in zip(s, slots)]
        back = [split(dot3(x, y, NN)) for x, y in zip(g, b)]
        term_b = [dot3(x, y, TN) for x, y in zip(g, p)]
        term_a = [dot3(x, y, NT) for x, y in zip(back, m)]
        term_r = [dot3(x, y, TN) for x, y in zip(a, back)]
        for (ta, tb, kind), x, y, z in zip(work, term_a, term_b, term_r):
            grads[rows(ta), :] += x
            grads[rows(tb), :] += y
            grad_r[kind] += z
        return carry

    lax.fori_loop(0, (jobs + TOGETHER - 1) // TOGETHER, group, 0)

    def each_kind(act):
        for kind in range(kinds_count):
            if rel is None:
                act(store_kind(kind))
            else:
                pl.when(seen[kind_at + kind] == 2)(functools.partial(act, store_kind(kind)))

    each_kind(lambda copy: copy.start())
    if first:
        each_unseen(per_part, tiles, lambda t: (load_right(t).wait(), store_right(t).start()) and None)
    if last:
        def settle_handed(t, carry):
            arrive_left(t)
            return carry

        lax.fori_loop(0, tiles, settle_handed, 0)
        if fill:
            each_unseen(tiles, 0, lambda t: (load_left(t).wait(), store_left(t).start()) and None)

    for copy in load_states:
        copy.wait()

    def update(j, carry):
        places = [order[j * UPDATES + n] for n in range(UPDATES)]
        done = [adagrad_tile(held[rows(at), :], states[pl.ds(at, 1), :], grads[rows(at), :]) for at in places]
        for at, (new, state_new) in zip(places, done):
            held[rows(at), :] = new
            states[pl.ds(at, 1), :] = state_new
            if last:
                pl.when(at < tiles)(lambda: store_left(at).start())
            pl.when((at >= tiles) & (at < spare))(lambda: store_right(at - tiles).start())
        return carry

    def each_touched(side_count, base, act):
        def body(t, carry):
            pl.when(seen[base + t] == 2)(lambda: act(t))
            return carry

        lax.fori_loop(0, side_count, body, 0)

    if not last:
        each_touched(tiles, 0, lambda t: hand(t).start())
    lax.fori_loop(0, (used + UPDATES - 1) // UPDATES, update, 0)
    for copy in store_states:
        copy.start()
    if not last:
        each_touched(tiles, 0, lambda t: hand(t).wait())
    else:
        each_touched(tiles, 0, lambda t: store_left(t).wait())
    each_touched(per_part, tiles, lambda t: store_right(t).wait())
    if fill:
        each_unseen(tiles, 0, lambda t: store_left(t).wait())
    if first:
        each_unseen(per_part, tiles, lambda t: store_right(t).wait())
    for copy in store_states:
        copy.wait()
    each_kind(lambda copy: copy.wait())


def run_part(turn, part, edges, lefts, rights, kinds, count, left, state_l, right, state_r, operators, rel, handed):
    first, last = state_r is not None, part == PARTS - 1
    anywhere = pl.BlockSpec(memory_space=pl.ANY)
    smem = pl.BlockSpec(memory_space=pltpu.SMEM)
    slots, tile = edges.shape[2], edges.shape[3]
    tiles, width = state_l.shape[0], left.shape[1]
    per_part = tiles // PARTS
    kinds_count = operators.shape[0]
    rows = (tiles + per_part + 1) * tile
    dma = pltpu.SemaphoreType.DMA
    shape = lambda *dims: jax.ShapeDtypeStruct(dims, F32)
    names = [("lefts", lefts), ("rights", rights), ("kinds", kinds), ("count", count), ("edges", edges), ("left", left)]
    names += [("state_l", state_l)] if last else []
    names += [("right", right)]
    names += [("state_r", state_r)] if first else []
    names += [("operators", operators)]
    names += [("rel", rel)] if rel is not None else []
    names += [("handed", handed)] if last else []
    outs = [("left", shape(*left.shape)), ("state_l", shape(*state_l.shape))] if last else []
    outs += [("right", shape(per_part * (tile + 1), width)), ("rel", shape(*operators.shape))]
    outs += [] if last else [("handed", shape(*left.shape))]
    place = {name: i for i, (name, _) in enumerate(names)}
    shared = {
        place[name]: i for i, (name, _) in enumerate(outs)
        if name in place and (name == "rel" or not first)
    }
    new = pl.pallas_call(
        functools.partial(bucket_kernel, turn, part, first, (tiles, per_part, tile, width, kinds_count)),
        in_specs=[smem] * 4 + [anywhere] * (len(names) - 4),
        out_specs=[anywhere] * len(outs),
        out_shape=[out for _, out in outs],
        input_output_aliases=shared,
        scratch_shapes=[
            pltpu.VMEM((slots, tile, tile), jnp.int32),
            pltpu.VMEM((rows, width), F32),
            pltpu.VMEM((rows, width), F32),
            pltpu.VMEM((tiles + per_part + 8, tile), F32),
            pltpu.VMEM(operators.shape, F32),
            pltpu.VMEM(operators.shape, BF16),
            pltpu.VMEM(operators.shape, BF16),
            pltpu.VMEM(operators.shape, F32),
            pltpu.SMEM((tiles + per_part + kinds_count,), jnp.int32),
            pltpu.SMEM((tiles + per_part + UPDATES,), jnp.int32),
            pltpu.SMEM((slots,), jnp.int32),
            dma((slots,)),
            dma((tiles + per_part,)),
            dma((tiles,)),
            dma((2, kinds_count)),
            dma((2,)),
        ],
        compiler_params=pltpu.CompilerParams(vmem_limit_bytes=63 * 1024 * 1024),
        cost_estimate=pl.CostEstimate(flops=4 * 10**9, bytes_accessed=4 * left.size, transcendentals=0),
    )(*[value for _, value in names])
    return dict(zip([name for name, _ in outs], new))


def unpack_kernel(layout, *refs):
    pieces, (table, state), (sems,) = refs[: len(layout)], refs[len(layout) : len(layout) + 2], refs[len(layout) + 2 :]
    body = table.shape[0] // PARTS
    per_part, tile = state.shape[0] // PARTS, state.shape[1]
    copies = []
    for (part, start, stop), piece in zip(layout, pieces):
        rows = min(stop, body) - start
        to = table.at[pl.ds(part * body + start, rows)]
        copies.append(pltpu.make_async_copy(piece.at[pl.ds(0, rows)], to, sems.at[len(copies)]))
        if stop > body:
            of = piece.at[pl.ds(rows, per_part), pl.ds(0, tile)]
            to = state.at[pl.ds(part * per_part, per_part)]
            copies.append(pltpu.make_async_copy(of, to, sems.at[len(copies)]))
    for copy in copies:
        copy.start()
    for copy in copies:
        copy.wait()


def unpack(layout, pieces, table, state):
    return pl.pallas_call(
        functools.partial(unpack_kernel, layout),
        in_specs=[pl.BlockSpec(memory_space=pltpu.VMEM)] * len(pieces),
        out_specs=[pl.BlockSpec(memory_space=pl.ANY)] * 2,
        out_shape=[jax.ShapeDtypeStruct(table, F32), jax.ShapeDtypeStruct(state, F32)],
        scratch_shapes=[pltpu.SemaphoreType.DMA((2 * len(pieces),))],
        compiler_params=pltpu.CompilerParams(vmem_limit_bytes=16 * 1024 * 1024),
    )(*pieces)


def shifted(block, axis, distance):
    n = lax.axis_size(axis)
    return lax.ppermute(block, axis, [(i, (i + distance) % n) for i in range(n)])


def sum_over(block, axis, sends, distance):
    n = lax.axis_size(axis)
    bits = n.bit_length() - 1
    if n != 1 << bits or block.shape[0] % n:
        return lax.psum(block, axis), [shifted(x, axis, distance) for x in sends]
    me = lax.axis_index(axis)
    digits, at = [], 0
    while at < bits:
        wide = 1 if at == 0 else min(2, bits - at)
        digits.append((at, 1 << wide))
        at += wide
    sends, arrived = list(sends), {0: shifted(sends[0], axis, distance)}
    plan = iter([((), ()), ((1,), (0,)), ((2,), (1,)), ((), (2,))])

    def tie(block):
        send, want = next(plan, ((), ()))
        for which in send:
            block, sends[which] = lax.optimization_barrier((block, sends[which]))
            arrived[which] = shifted(sends[which], axis, distance)
        for which in want:
            block, arrived[which] = lax.optimization_barrier((block, arrived[which]))
        return block

    def partners(at, size):
        return [[(i, i ^ (j << at)) for i in range(n)] for j in range(1, size)]

    *scattered, (last_at, last_size) = digits
    for at, size in scattered:
        block = tie(block)
        mine = (me >> at) & (size - 1)
        parts = block.reshape(size, -1, block.shape[1])
        got = [
            lax.ppermute(lax.dynamic_index_in_dim(parts, mine ^ j, keepdims=False), axis, route)
            for j, route in enumerate(partners(at, size), 1)
        ]
        block = lax.dynamic_index_in_dim(parts, mine, keepdims=False)
        for other in got:
            block = block + other
    block = tie(block)
    terms = [block] + [lax.ppermute(block, axis, route) for route in partners(last_at, last_size)]
    while len(terms) > 1:
        terms = [a + b for a, b in zip(terms[::2], terms[1::2])]
    block = terms[0]
    for at, size in reversed(scattered):
        block = tie(block)
        mine = (me >> at) & (size - 1)
        got = [block] + [lax.ppermute(block, axis, route) for route in partners(at, size)]
        whole = jnp.zeros((size,) + block.shape, block.dtype)
        for j, other in enumerate(got):
            whole = lax.dynamic_update_index_in_dim(whole, other, mine ^ j, 0)
        block = whole.reshape(-1, block.shape[1])
    tie(block)
    return block, [arrived.get(i) if i in arrived else shifted(x, axis, distance) for i, x in enumerate(sends)]


def adagrad_rows(table, state, grad):
    state_new = state + jnp.mean(grad * grad, axis=1)
    return table - learn_rate * grad / (jnp.sqrt(state_new)[:, None] + epsilon), state_new


def per_device(
    left_table, left_state, right_table, right_state, relations, relation_state,
    edge_weights, tile_left, tile_right, tile_relation, live_count,
):
    rounds, tile = edge_weights.shape[1], edge_weights.shape[-1]
    left, state_l = left_table, left_state.reshape(-1, tile)
    rights_now = [right_table] * PARTS
    state_r = right_state.reshape(-1, tile)
    rel = None
    for turn in range(rounds):
        handed = None
        for part in range(PARTS):
            new = run_part(
                turn, part, edge_weights, tile_left, tile_right, tile_relation, live_count,
                left, state_l, rights_now[part], state_r if turn == 0 else None, relations, rel, handed,
            )
            rel, handed = new["rel"], new.get("handed")
            rights_now[part] = shifted(new["right"], "dev", 1) if turn + 1 < rounds else new["right"]
        left, state_l = new["left"], new["state_l"]
    width = relations.shape[-1]
    rows = rights_now[0].shape[0]
    cut = rows // 2 // 8 * 8
    cuts = [(0, 0, rows)] + [(1, start, stop) for start, stop in zip((0, cut), (cut, rows))]
    pieces = [rights_now[0]] + [lax.slice_in_dim(rights_now[1], start, stop) for _, start, stop in cuts[1:]]
    total, pieces = sum_over(rel.reshape(-1, width), "dev", pieces, 1 - rounds)
    right, state_r = unpack(cuts, pieces, right_table.shape, (right_state.shape[0] // tile, tile))
    new_rel, new_state = adagrad_rows(relations.reshape(-1, width), relation_state.reshape(-1), total)
    return (
        left, state_l.reshape(left_state.shape), right, state_r.reshape(right_state.shape),
        new_rel.reshape(relations.shape), new_state.reshape(relation_state.shape),
    )


def solution(mesh):
    placed = (
        P("dev", None), P("dev"), P("dev", None), P("dev"), P(), P(),
        P("dev", None, None, None, None), P("dev", None, None), P("dev", None, None), P("dev", None, None),
        P("dev", None),
    )
    return jax.shard_map(
        per_device, mesh=mesh, in_specs=placed,
        out_specs=(P("dev", None), P("dev"), P("dev", None), P("dev"), P(), P()), check_vma=False,
    )
```

```python
import functools

import jax
import jax.numpy as jnp
from jax import lax
from jax.experimental import pallas as pl
from jax.experimental.pallas import tpu as pltpu
from jax.sharding import PartitionSpec as P

learn_rate = 0.1
epsilon = 1e-06
weight_scale = 3.0

F32 = jnp.float32
BF16 = jnp.bfloat16
PARTS = 2
WAYS = ((0, 1), (0,), (1,))
TOGETHER = 4
UPDATES = 8

NN = ((1,), (0,))
NT = ((1,), (1,))
TN = ((0,), (0,))


def split(value):
    high = value.astype(BF16)
    return high, (value - high.astype(F32)).astype(BF16)


def dot3(a, b, dims):
    (ah, al), (bh, bl) = a, b
    ca, cb = dims[0][0], dims[1][0]
    return lax.dot_general(
        jnp.concatenate([ah, ah, al], axis=ca),
        jnp.concatenate([bh, bl, bh], axis=cb),
        (dims, ((), ())),
        preferred_element_type=F32,
    )


def dscore(s, w, scale):
    small = jnp.exp(-jnp.abs(s))
    large_part = 1.0 / (1.0 + small)
    small_part = small * large_part
    up = s >= 0
    sig = jnp.where(up, large_part, small_part)
    anti = jnp.where(up, small_part, large_part)
    return jnp.where(w == 0, sig, anti * (w.astype(F32) * (-1.0 / weight_scale))) * scale


def adagrad_tile(table, state_row, grad):
    tile, width = grad.shape
    eye = lax.broadcasted_iota(jnp.int32, (tile, tile), 0) == lax.broadcasted_iota(jnp.int32, (tile, tile), 1)
    mean = jnp.sum(grad * grad, axis=1, keepdims=True) / width
    state_new = state_row + jnp.sum(jnp.where(eye, mean, 0.0), axis=0, keepdims=True)
    rate_row = learn_rate / (jnp.sqrt(state_new) + epsilon)
    rate = jnp.sum(jnp.where(eye, rate_row, 0.0), axis=1, keepdims=True)
    return table - grad * rate, state_new


def bucket_kernel(turn, part, first, dims, lefts, rights, kinds, count, edges, *refs):
    tiles, per_part, tile, width, kinds_count = dims
    last = part == PARTS - 1
    refs = list(refs)
    left = refs.pop(0)
    state_l = refs.pop(0) if last else None
    right = refs.pop(0)
    state_r = refs.pop(0) if first else None
    operators = refs.pop(0)
    rel = None if first and part == 0 else refs.pop(0)
    handed = refs.pop(0) if last else None
    if last:
        left_out, state_l_out = refs.pop(0), refs.pop(0)
    right_out, rel_out = refs.pop(0), refs.pop(0)
    handed_out = None if last else refs.pop(0)
    (weights, held, grads, states, maps, highs, lows, grad_r, seen, order, todo, sem_w, sem_t, sem_g, sem_k, sem_s) = refs
    fill = first and last
    scale = width ** (-0.5)
    live = count[0, turn]
    spare = tiles + per_part
    kind_at = spare

    def rows(t):
        return pl.ds(pl.multiple_of(t * tile, tile), tile)

    def load_left(t):
        return pltpu.make_async_copy(left.at[rows(t)], held.at[rows(t)], sem_t.at[t])

    def store_left(t):
        return pltpu.make_async_copy(held.at[rows(t)], left_out.at[rows(t)], sem_t.at[t])

    def load_right(t):
        at = tiles + t
        source = right.at[rows(part * per_part + t)] if first else right.at[rows(t)]
        return pltpu.make_async_copy(source, held.at[rows(at)], sem_t.at[at])

    def store_right(t):
        at = tiles + t
        return pltpu.make_async_copy(held.at[rows(at)], right_out.at[rows(t)], sem_t.at[at])

    def take(t):
        return pltpu.make_async_copy(handed.at[rows(t)], grads.at[rows(t)], sem_g.at[t])

    def hand(t):
        return pltpu.make_async_copy(grads.at[rows(t)], handed_out.at[rows(t)], sem_g.at[t])

    def load_weights(i):
        return pltpu.make_async_copy(edges.at[0, turn, i], weights.at[i], sem_w.at[i])

    def load_kind(kind):
        copies = [pltpu.make_async_copy(operators.at[kind], maps.at[kind], sem_k.at[0, kind])]
        if rel is not None:
            copies.append(pltpu.make_async_copy(rel.at[kind], grad_r.at[kind], sem_k.at[1, kind]))
        return copies

    def store_kind(kind):
        return pltpu.make_async_copy(grad_r.at[kind], rel_out.at[kind], sem_k.at[1, kind])

    held_r = states.at[pl.ds(tiles, per_part)]
    packed = pl.ds(per_part * tile, per_part), pl.ds(0, tile)
    source = state_r.at[pl.ds(part * per_part, per_part)] if first else right.at[packed]
    load_states = [pltpu.make_async_copy(source, held_r, sem_s.at[0])]
    store_states = [pltpu.make_async_copy(held_r, right_out.at[packed], sem_s.at[0])]
    if last:
        held_l = states.at[pl.ds(0, tiles)]
        load_states.append(pltpu.make_async_copy(state_l, held_l, sem_s.at[1]))
        store_states.append(pltpu.make_async_copy(held_l, state_l_out, sem_s.at[1]))

    for t in range(spare + kinds_count):
        seen[t] = 0
    for t in range(spare + UPDATES):
        order[t] = spare
    used = jnp.int32(0)

    def mine(i):
        return rights[0, turn, i] // per_part == part

    def ask(i, carry):
        used, jobs = carry
        now = mine(i)
        a, b, kind = lefts[0, turn, i], rights[0, turn, i] - part * per_part, kinds[0, turn, i]
        new_a = now & (seen[a] == 0)
        new_b = now & (seen[jnp.where(now, tiles + b, 0)] == 0)

        @pl.when(now)
        def _():
            todo[jobs] = i
            load_weights(i).start()

            @pl.when(seen[kind_at + kind] == 0)
            def _():
                for copy in load_kind(kind):
                    copy.start()
                seen[kind_at + kind] = 1

        @pl.when(new_a)
        def _():
            load_left(a).start()
            seen[a] = 1
            grads[rows(a), :] = jnp.zeros((tile, width), F32)
            if last:
                order[used] = a

        if last:
            used = used + new_a.astype(jnp.int32)

        @pl.when(new_b)
        def _():
            load_right(b).start()
            seen[tiles + b] = 1
            grads[rows(tiles + b), :] = jnp.zeros((tile, width), F32)
            order[used] = tiles + b

        return used + new_b.astype(jnp.int32), jobs + now.astype(jnp.int32)

    if last:
        def ask_handed(i, used):
            a = lefts[0, turn, i]
            new = jnp.logical_not(mine(i)) & (seen[a] == 0)

            @pl.when(new)
            def _():
                load_left(a).start()
                take(a).start()
                seen[a] = 4
                order[used] = a

            return used + new.astype(jnp.int32)

        used = lax.fori_loop(0, live, ask_handed, used)
    used, jobs = lax.fori_loop(0, live, ask, (used, jnp.int32(0)))
    states[pl.ds(spare, 8), :] = jnp.ones((8, tile), F32)
    for copy in load_states:
        copy.start()
    if rel is None:
        grad_r[...] = jnp.zeros_like(grad_r)

    def each_unseen(side_count, base, act):
        def body(t, carry):
            pl.when(seen[base + t] == 0)(lambda: act(t))
            return carry

        lax.fori_loop(0, side_count, body, 0)

    if fill:
        each_unseen(tiles, 0, lambda t: load_left(t).start())
    if first:
        each_unseen(per_part, tiles, lambda t: load_right(t).start())
    held[rows(spare), :] = jnp.zeros((tile, width), F32)
    grads[rows(spare), :] = jnp.zeros((tile, width), F32)

    def arrive_left(a):
        @pl.when(seen[a] == 1)
        def _():
            load_left(a).wait()
            seen[a] = 2

        if last:
            @pl.when(seen[a] == 4)
            def _():
                load_left(a).wait()
                take(a).wait()
                seen[a] = 2

    def arrive(i):
        arrive_left(lefts[0, turn, i])
        b, kind = rights[0, turn, i] - part * per_part, kinds[0, turn, i]

        @pl.when(seen[tiles + b] == 1)
        def _():
            load_right(b).wait()
            seen[tiles + b] = 2

        @pl.when(seen[kind_at + kind] == 1)
        def _():
            for copy in load_kind(kind):
                copy.wait()
            highs[kind], lows[kind] = split(maps[kind])
            seen[kind_at + kind] = 2

        load_weights(i).wait()

    def group(j, carry):
        places = [j * TOGETHER + n for n in range(TOGETHER)]
        slots = [todo[jnp.minimum(place, jobs - 1)] for place in places]
        arrive(slots[0])
        for i, place in zip(slots[1:], places[1:]):
            pl.when(place < jobs)(functools.partial(arrive, i))
        work = [
            (
                jnp.where(place < jobs, lefts[0, turn, i], spare),
                jnp.where(place < jobs, tiles + rights[0, turn, i] - part * per_part, spare),
                kinds[0, turn, i],
            )
            for i, place in zip(slots, places)
        ]
        a = [split(held[rows(ta), :]) for ta, _, _ in work]
        b = [split(held[rows(tb), :]) for _, tb, _ in work]
        m = [(highs[kind], lows[kind]) for _, _, kind in work]
        p = [split(dot3(x, y, NN)) for x, y in zip(a, m)]
        s = [dot3(x, y, NT) * scale for x, y in zip(p, b)]
        g = [split(dscore(x, weights[i], scale)) for x, i in zip(s, slots)]
        back = [split(dot3(x, y, NN)) for x, y in zip(g, b)]
        term_b = [dot3(x, y, TN) for x, y in zip(g, p)]
        term_a = [dot3(x, y, NT) for x, y in zip(back, m)]
        term_r = [dot3(x, y, TN) for x, y in zip(a, back)]
        for (ta, tb, kind), x, y, z in zip(work, term_a, term_b, term_r):
            grads[rows(ta), :] += x
            grads[rows(tb), :] += y
            grad_r[kind] += z
        return carry

    lax.fori_loop(0, (jobs + TOGETHER - 1) // TOGETHER, group, 0)

    def each_kind(act):
        for kind in range(kinds_count):
            if rel is None:
                act(store_kind(kind))
            else:
                pl.when(seen[kind_at + kind] == 2)(functools.partial(act, store_kind(kind)))

    each_kind(lambda copy: copy.start())
    if first:
        each_unseen(per_part, tiles, lambda t: (load_right(t).wait(), store_right(t).start()) and None)
    if last:
        def settle_handed(t, carry):
            arrive_left(t)
            return carry

        lax.fori_loop(0, tiles, settle_handed, 0)
        if fill:
            each_unseen(tiles, 0, lambda t: (load_left(t).wait(), store_left(t).start()) and None)

    for copy in load_states:
        copy.wait()

    def update(j, carry):
        places = [order[j * UPDATES + n] for n in range(UPDATES)]
        done = [adagrad_tile(held[rows(at), :], states[pl.ds(at, 1), :], grads[rows(at), :]) for at in places]
        for at, (new, state_new) in zip(places, done):
            held[rows(at), :] = new
            states[pl.ds(at, 1), :] = state_new
            if last:
                pl.when(at < tiles)(lambda: store_left(at).start())
            pl.when((at >= tiles) & (at < spare))(lambda: store_right(at - tiles).start())
        return carry

    def each_touched(side_count, base, act):
        def body(t, carry):
            pl.when(seen[base + t] == 2)(lambda: act(t))
            return carry

        lax.fori_loop(0, side_count, body, 0)

    if not last:
        each_touched(tiles, 0, lambda t: hand(t).start())
    lax.fori_loop(0, (used + UPDATES - 1) // UPDATES, update, 0)
    for copy in store_states:
        copy.start()
    if not last:
        each_touched(tiles, 0, lambda t: hand(t).wait())
    else:
        each_touched(tiles, 0, lambda t: store_left(t).wait())
    each_touched(per_part, tiles, lambda t: store_right(t).wait())
    if fill:
        each_unseen(tiles, 0, lambda t: store_left(t).wait())
    if first:
        each_unseen(per_part, tiles, lambda t: store_right(t).wait())
    for copy in store_states:
        copy.wait()
    each_kind(lambda copy: copy.wait())


def run_part(turn, part, edges, lefts, rights, kinds, count, left, state_l, right, state_r, operators, rel, handed):
    first, last = state_r is not None, part == PARTS - 1
    anywhere = pl.BlockSpec(memory_space=pl.ANY)
    smem = pl.BlockSpec(memory_space=pltpu.SMEM)
    slots, tile = edges.shape[2], edges.shape[3]
    tiles, width = state_l.shape[0], left.shape[1]
    per_part = tiles // PARTS
    kinds_count = operators.shape[0]
    rows = (tiles + per_part + 1) * tile
    dma = pltpu.SemaphoreType.DMA
    shape = lambda *dims: jax.ShapeDtypeStruct(dims, F32)
    names = [("lefts", lefts), ("rights", rights), ("kinds", kinds), ("count", count), ("edges", edges), ("left", left)]
    names += [("state_l", state_l)] if last else []
    names += [("right", right)]
    names += [("state_r", state_r)] if first else []
    names += [("operators", operators)]
    names += [("rel", rel)] if rel is not None else []
    names += [("handed", handed)] if last else []
    outs = [("left", shape(*left.shape)), ("state_l", shape(*state_l.shape))] if last else []
    outs += [("right", shape(per_part * (tile + 1), width)), ("rel", shape(*operators.shape))]
    outs += [] if last else [("handed", shape(*left.shape))]
    place = {name: i for i, (name, _) in enumerate(names)}
    shared = {
        place[name]: i for i, (name, _) in enumerate(outs)
        if name in place and (name == "rel" or not first)
    }
    new = pl.pallas_call(
        functools.partial(bucket_kernel, turn, part, first, (tiles, per_part, tile, width, kinds_count)),
        in_specs=[smem] * 4 + [anywhere] * (len(names) - 4),
        out_specs=[anywhere] * len(outs),
        out_shape=[out for _, out in outs],
        input_output_aliases=shared,
        scratch_shapes=[
            pltpu.VMEM((slots, tile, tile), jnp.int32),
            pltpu.VMEM((rows, width), F32),
            pltpu.VMEM((rows, width), F32),
            pltpu.VMEM((tiles + per_part + 8, tile), F32),
            pltpu.VMEM(operators.shape, F32),
            pltpu.VMEM(operators.shape, BF16),
            pltpu.VMEM(operators.shape, BF16),
            pltpu.VMEM(operators.shape, F32),
            pltpu.SMEM((tiles + per_part + kinds_count,), jnp.int32),
            pltpu.SMEM((tiles + per_part + UPDATES,), jnp.int32),
            pltpu.SMEM((slots,), jnp.int32),
            dma((slots,)),
            dma((tiles + per_part,)),
            dma((tiles,)),
            dma((2, kinds_count)),
            dma((2,)),
        ],
        compiler_params=pltpu.CompilerParams(vmem_limit_bytes=63 * 1024 * 1024),
        cost_estimate=pl.CostEstimate(flops=4 * 10**9, bytes_accessed=4 * left.size, transcendentals=0),
    )(*[value for _, value in names])
    return dict(zip([name for name, _ in outs], new))


def unpack_kernel(turn, *refs):
    pieces, (table, state), (sems,) = refs[: PARTS + 1], refs[PARTS + 1 : PARTS + 3], refs[PARTS + 3 :]
    body = table.shape[0] // PARTS
    per_part, tile = state.shape[0] // PARTS, state.shape[1]

    def copies(part, piece):
        states = piece.at[pl.ds(body, per_part), pl.ds(0, tile)]
        return (
            pltpu.make_async_copy(piece.at[pl.ds(0, body)], table.at[pl.ds(part * body, body)], sems.at[2 * part]),
            pltpu.make_async_copy(states, state.at[pl.ds(part * per_part, per_part)], sems.at[2 * part + 1]),
        )

    def each(act):
        for part in range(PARTS - 1):
            for copy in copies(part, pieces[part]):
                act(copy)
        for way in (0, 1):
            @pl.when(turn[0] == way)
            def _():
                for copy in copies(PARTS - 1, pieces[PARTS - 1 + way]):
                    act(copy)

    each(lambda copy: copy.start())
    each(lambda copy: copy.wait())


def unpack(turn, pieces, table, state):
    return pl.pallas_call(
        unpack_kernel,
        in_specs=[pl.BlockSpec(memory_space=pltpu.SMEM)] + [pl.BlockSpec(memory_space=pltpu.VMEM)] * len(pieces),
        out_specs=[pl.BlockSpec(memory_space=pl.ANY)] * 2,
        out_shape=[jax.ShapeDtypeStruct(table, F32), jax.ShapeDtypeStruct(state, F32)],
        scratch_shapes=[pltpu.SemaphoreType.DMA((2 * PARTS,))],
        compiler_params=pltpu.CompilerParams(vmem_limit_bytes=16 * 1024 * 1024),
    )(turn, *pieces)


def shifted(block, axis, distance, senders=(0, 1)):
    n = lax.axis_size(axis)
    return lax.ppermute(block, axis, [(i, (i + distance) % n) for i in range(n) if i % 2 in senders])


def sum_over(block, axis, sends, distance):
    n = lax.axis_size(axis)
    bits = n.bit_length() - 1
    if n != 1 << bits or block.shape[0] % n:
        return lax.psum(block, axis), [shifted(x, axis, distance, way) for x, way in zip(sends, WAYS)]
    me = lax.axis_index(axis)
    digits, at = [], 0
    while at < bits:
        wide = 1 if at == 0 else min(2, bits - at)
        digits.append((at, 1 << wide))
        at += wide
    sends, arrived = list(sends), {0: shifted(sends[0], axis, distance)}
    plan = iter([((), ()), ((1,), (0,)), ((2,), ()), ((), (1,)), ((), (2,))])

    def tie(block):
        send, want = next(plan, ((), ()))
        for which in send:
            block, sends[which] = lax.optimization_barrier((block, sends[which]))
            arrived[which] = shifted(sends[which], axis, distance, WAYS[which])
        for which in want:
            block, arrived[which] = lax.optimization_barrier((block, arrived[which]))
        return block

    def partners(at, size):
        return [[(i, i ^ (j << at)) for i in range(n)] for j in range(1, size)]

    *scattered, (last_at, last_size) = digits
    for at, size in scattered:
        block = tie(block)
        mine = (me >> at) & (size - 1)
        parts = block.reshape(size, -1, block.shape[1])
        got = [
            lax.ppermute(lax.dynamic_index_in_dim(parts, mine ^ j, keepdims=False), axis, route)
            for j, route in enumerate(partners(at, size), 1)
        ]
        block = lax.dynamic_index_in_dim(parts, mine, keepdims=False)
        for other in got:
            block = block + other
    block = tie(block)
    terms = [block] + [lax.ppermute(block, axis, route) for route in partners(last_at, last_size)]
    while len(terms) > 1:
        terms = [a + b for a, b in zip(terms[::2], terms[1::2])]
    block = terms[0]
    for at, size in reversed(scattered):
        block = tie(block)
        mine = (me >> at) & (size - 1)
        got = [block] + [lax.ppermute(block, axis, route) for route in partners(at, size)]
        whole = jnp.zeros((size,) + block.shape, block.dtype)
        for j, other in enumerate(got):
            whole = lax.dynamic_update_index_in_dim(whole, other, mine ^ j, 0)
        block = whole.reshape(-1, block.shape[1])
    tie(block)
    return block, [arrived.get(i) if i in arrived else shifted(x, axis, distance, WAYS[i]) for i, x in enumerate(sends)]


def adagrad_rows(table, state, grad):
    state_new = state + jnp.mean(grad * grad, axis=1)
    return table - learn_rate * grad / (jnp.sqrt(state_new)[:, None] + epsilon), state_new


def per_device(
    left_table, left_state, right_table, right_state, relations, relation_state,
    edge_weights, tile_left, tile_right, tile_relation, live_count,
):
    rounds, tile = edge_weights.shape[1], edge_weights.shape[-1]
    left, state_l = left_table, left_state.reshape(-1, tile)
    rights_now = [right_table] * PARTS
    state_r = right_state.reshape(-1, tile)
    rel = None
    for turn in range(rounds):
        handed = None
        for part in range(PARTS):
            new = run_part(
                turn, part, edge_weights, tile_left, tile_right, tile_relation, live_count,
                left, state_l, rights_now[part], state_r if turn == 0 else None, relations, rel, handed,
            )
            rel, handed = new["rel"], new.get("handed")
            rights_now[part] = shifted(new["right"], "dev", 1) if turn + 1 < rounds else new["right"]
        left, state_l = new["left"], new["state_l"]
    width = relations.shape[-1]
    sends = [rights_now[0], rights_now[1], rights_now[1]]
    total, pieces = sum_over(rel.reshape(-1, width), "dev", sends, 1 - rounds)
    way = lax.rem(lax.axis_index("dev") + rounds - 1, 2).reshape(1)
    right, state_r = unpack(way, pieces, right_table.shape, (right_state.shape[0] // tile, tile))
    new_rel, new_state = adagrad_rows(relations.reshape(-1, width), relation_state.reshape(-1), total)
    return (
        left, state_l.reshape(left_state.shape), right, state_r.reshape(right_state.shape),
        new_rel.reshape(relations.shape), new_state.reshape(relation_state.shape),
    )


def solution(mesh):
    placed = (
        P("dev", None), P("dev"), P("dev", None), P("dev"), P(), P(),
        P("dev", None, None, None, None), P("dev", None, None), P("dev", None, None), P("dev", None, None),
        P("dev", None),
    )
    return jax.shard_map(
        per_device, mesh=mesh, in_specs=placed,
        out_specs=(P("dev", None), P("dev"), P("dev", None), P("dev"), P(), P()), check_vma=False,
    )
```
